128 devices in a mesh: tm: 16 (over y, x), patch: 8 (over z, core).
Axes of the slice: x: 4, y: 4, z: 4, core: 2. Of those that a mesh axis runs over, the one named last changes fastest.
Arguments:
- snapshots: bfloat16 [128, 8192, 256], P('tm', 'patch'), may hold values from -6 to 6
- neighbours: int32 [8192, 5], P('patch'), may hold values from 0 to 8191, as said below
- owners: int32 [8192], P('patch'), may hold values from 0 to 2047, as said below
- w_mix1: bfloat16 [1280, 256], replicated, may hold values from -0.15625 to 0.15625
- w_mix2: bfloat16 [256, 256], replicated, may hold values from -0.375 to 0.375
- w_lift: bfloat16 [256, 512], replicated, may hold values from -0.375 to 0.375
- gain_attn: float32 [512], replicated, may hold values from 0.5 to 10
- w_qkv: bfloat16 [512, 1536], replicated, may hold values from -0.25 to 0.25
- w_out: bfloat16 [512, 512], replicated, may hold values from -0.25 to 0.25
- gain_ffn: float32 [512], replicated, may hold values from 0.1 to 1.9
- w_gate: bfloat16 [512, 2048], replicated, may hold values from -0.25 to 0.25
- w_up: bfloat16 [512, 2048], replicated, may hold values from -0.25 to 0.25
- w_down: bfloat16 [2048, 512], replicated, may hold values from -0.125 to 0.125
- w_dec: bfloat16 [512, 256], replicated, may hold values from -0.25 to 0.25
Outputs:
- decoded: bfloat16 [128, 8192, 256], P('tm', 'patch')
The draws below stay inside these ranges and needn't reach their ends.
Inputs may be any that keep to these rules, and one draw needn't show every extreme that they name: neighbours[e, 0] is e; every entry lies within 64 of e in edge order and inside 0 to 8191; some entries lie exactly 64 away. owners[e] for an edge of patch p (edges 1024 * p to 1024 * (p + 1) - 1) is a coarse edge of that patch, 256 * p to 256 * (p + 1) - 1; every coarse edge is named by one or more fine edges.
All inputs are finite; a program needn't handle non-finite values.
Results may differ from the reference program's by a relative error of at most 0.04.
The reference program's roundings to bfloat16 on the way count: a program that leaves them out, or rounds other values in their place, can miss the bound.
Values may be sent and summed in bfloat16 or wider, within the bound.
No kernel may reach another device: no remote copies, remote signals or barrier semaphores. Data moves between devices by JAX's collectives and lax.ppermute only.
A program may use at most 192 MiB of HBM per device.

```python
import jax
import jax.numpy as jnp
from jax import lax

C = 256
DC = 512
HEADS = 8
FFN = 2048
HALO = 64
E_DEV = 1024
CC_DEV = 256
SNAPS = 128
EDGES = 8192
COARSE = 2048


def draw_neighbours(key, part):
    edge_ids = jnp.arange(EDGES, dtype=jnp.int32)
    offsets = jax.random.randint(key, (EDGES, 5), -HALO, HALO + 1).astype(jnp.int32)
    signs = jax.random.randint(jax.random.fold_in(key, 11), (EDGES,), 0, 2).astype(jnp.int32) * 2 - 1
    far_col = jnp.where(edge_ids % 32 == 0, signs * HALO, offsets[:, 4])
    offsets = offsets.at[:, 4].set(far_col)
    offsets = offsets.at[:, 0].set(0)
    return jnp.clip(edge_ids[:, None] + offsets, 0, EDGES - 1).astype(jnp.int32)


def draw_owners(key, part):
    patches = EDGES // E_DEV

    def one_patch(index):
        patch_key = jax.random.fold_in(key, index + 101)
        order = jax.random.permutation(patch_key, E_DEV).astype(jnp.int32)
        first = jax.random.randint(jax.random.fold_in(patch_key, 1), (E_DEV,), 0, CC_DEV)
        second = jax.random.randint(jax.random.fold_in(patch_key, 2), (E_DEV,), 0, CC_DEV)
        spare = jnp.minimum(first, second).astype(jnp.int32)
        slot_ids = jnp.where(order < CC_DEV, order, spare)
        return slot_ids + index * CC_DEV
    return jax.vmap(one_patch)(jnp.arange(patches, dtype=jnp.int32)).reshape(EDGES).astype(jnp.int32)


def draw_gain_attn(key, part):
    return jax.random.uniform(key, (DC,), jnp.float32, 0.5, 1.5)


def levels(stream_key, shape, pieces, smallest, high):
    gain, own = 1.0, jax.random.fold_in(stream_key, 6)
    for dim, shards_of in pieces:
        steps = jnp.exp(jax.random.uniform(jax.random.fold_in(own, dim), (shards_of,), jnp.float32, smallest / len(pieces), high / len(pieces)))
        gain = gain * jnp.repeat(steps, shape[dim] // shards_of).reshape([-1 if axis == dim else 1 for axis in range(len(shape))])
    return gain


def centred(stream_key, dims, spread, most, pieces=(), kind=jnp.bfloat16):
    level = levels(stream_key, dims, pieces, -0.22, 0.18) if pieces else 1.0
    values = jax.random.normal(stream_key, dims, jnp.float32) * spread * level
    return jnp.minimum(jnp.maximum(values, -most), most).astype(kind)


def setup_inputs(seed: int = 0) -> dict:
    arg_keys = jax.random.split(jax.random.key(seed), 15)
    snapshots = centred(arg_keys[0], (SNAPS, EDGES, C), 1.0, 6.0, ((0, 16), (1, 8)))
    neighbours = draw_neighbours(jax.random.fold_in(arg_keys[14], 71), 0)
    owners = draw_owners(jax.random.fold_in(arg_keys[14], 71), 0)
    w_mix1 = centred(arg_keys[3], (5 * C, C), (5 * C) ** -0.5, 0.15625)
    w_mix2 = centred(arg_keys[4], (C, C), C ** -0.5, 0.375)
    w_lift = centred(arg_keys[5], (C, DC), C ** -0.5, 0.375)
    gain_attn = draw_gain_attn(jax.random.fold_in(arg_keys[14], 71), 0)
    w_qkv = centred(arg_keys[7], (DC, 3 * DC), DC ** -0.5, 0.25)
    w_out = centred(arg_keys[8], (DC, DC), DC ** -0.5, 0.25)
    gain_ffn = jnp.clip(1.0 + 0.18 * jax.random.normal(arg_keys[9], (DC,), jnp.float32), 0.1, 1.9)
    w_gate = centred(arg_keys[10], (DC, FFN), DC ** -0.5, 0.25)
    w_up = centred(arg_keys[11], (DC, FFN), DC ** -0.5, 0.25)
    w_down = centred(arg_keys[12], (FFN, DC), FFN ** -0.5, 0.125)
    w_dec = centred(arg_keys[13], (DC, C), DC ** -0.5, 0.25)
    return {"snapshots": snapshots, "neighbours": neighbours, "owners": owners, "w_mix1": w_mix1, "w_mix2": w_mix2, "w_lift": w_lift, "gain_attn": gain_attn, "w_qkv": w_qkv, "w_out": w_out, "gain_ffn": gain_ffn, "w_gate": w_gate, "w_up": w_up, "w_down": w_down, "w_dec": w_dec}


eps_norm = 1e-05

def rms_scale(rows_in, gain_vec):
    mean_sq = lax.optimization_barrier(jnp.mean(rows_in * rows_in, axis=-1, keepdims=True))
    return rows_in * lax.rsqrt(mean_sq + eps_norm) * gain_vec.astype(jnp.float32)

def project(rows_in, weight):
    lead_dims = rows_in.shape[:-1]
    flat_out = jnp.dot(rows_in.reshape(-1, rows_in.shape[-1]), weight, preferred_element_type=jnp.float32)
    return flat_out.reshape(lead_dims + (weight.shape[1],))

def temporal(state_in, gain_attn, w_qkv, w_out, gain_ffn, w_gate, w_up, w_down):
    steps_n, n_coarse, feat_width = state_in.shape
    head_size = feat_width // HEADS
    state_f = state_in.astype(jnp.float32)
    normed = rms_scale(state_f, gain_attn).astype(jnp.bfloat16)
    qkv = project(normed, w_qkv).astype(jnp.bfloat16)
    queries = qkv[..., :feat_width].reshape(steps_n, n_coarse, HEADS, head_size).astype(jnp.float32)
    key_rows = qkv[..., feat_width:2 * feat_width].reshape(steps_n, n_coarse, HEADS, head_size).astype(jnp.float32)
    value_rows = qkv[..., 2 * feat_width:].reshape(steps_n, n_coarse, HEADS, head_size).astype(jnp.float32)
    scores = jnp.einsum('tkhd,skhd->khts', queries, key_rows) * head_size ** (-0.5)
    causal = jnp.arange(steps_n)[:, None] >= jnp.arange(steps_n)[None, :]
    scores = jnp.where(causal, scores, -jnp.inf)
    weights = jax.nn.softmax(scores, axis=-1).astype(jnp.bfloat16)
    attended = jnp.einsum('khts,skhd->tkhd', weights.astype(jnp.float32), value_rows)
    attended = attended.astype(jnp.bfloat16).reshape(steps_n, n_coarse, feat_width)
    state_one = (state_f + project(attended, w_out)).astype(jnp.bfloat16)
    one_f = state_one.astype(jnp.float32)
    normed_two = rms_scale(one_f, gain_ffn).astype(jnp.bfloat16)
    gate_act = project(normed_two, w_gate)
    up_act = project(normed_two, w_up)
    hidden = (jax.nn.silu(gate_act) * up_act).astype(jnp.bfloat16)
    return (one_f + project(hidden, w_down)).astype(jnp.bfloat16)

def reference(snapshots, neighbours, owners, w_mix1, w_mix2, w_lift, gain_attn, w_qkv, w_out, gain_ffn, w_gate, w_up, w_down, w_dec):
    feat_width = snapshots.shape[2]

    def mix_edges(snapshot):
        gathered = snapshot[neighbours].reshape(EDGES, 5 * feat_width)
        activated = jax.nn.gelu(jnp.dot(gathered, w_mix1, preferred_element_type=jnp.float32)).astype(jnp.bfloat16)
        return (snapshot.astype(jnp.float32) + jnp.dot(activated, w_mix2, preferred_element_type=jnp.float32)).astype(jnp.bfloat16)
    mixed_fine = lax.map(mix_edges, snapshots)
    counts = jax.ops.segment_sum(jnp.ones((EDGES,), jnp.float32), owners, num_segments=COARSE)

    def pool_rows(snapshot):
        pool_sums = jax.ops.segment_sum(snapshot.astype(jnp.float32), owners, num_segments=COARSE)
        pooled = (pool_sums / counts[:, None]).astype(jnp.bfloat16)
        return jnp.dot(pooled, w_lift, preferred_element_type=jnp.float32).astype(jnp.bfloat16)
    lifted = lax.map(pool_rows, mixed_fine)
    coarse_blocks = lifted.reshape(SNAPS, COARSE // CC_DEV, CC_DEV, DC).transpose(1, 0, 2, 3)

    def run_layer(coarse_block):
        state_two = temporal(coarse_block, gain_attn, w_qkv, w_out, gain_ffn, w_gate, w_up, w_down)
        return project(state_two, w_dec).astype(jnp.bfloat16)
    coarse_out = lax.map(run_layer, coarse_blocks).transpose(1, 0, 2, 3).reshape(SNAPS, COARSE, feat_width)

    def unpool(paired):
        snapshot, coarse_row = paired
        return (snapshot.astype(jnp.float32) + coarse_row[owners].astype(jnp.float32)).astype(jnp.bfloat16)
    return lax.map(unpool, (mixed_fine, coarse_out))
```

```python
import functools

import jax
import jax.numpy as jnp
from jax import lax
from jax.experimental import pallas as pl
from jax.experimental.pallas import tpu as pltpu
from jax.sharding import PartitionSpec as P

HEADS = 8
HALO = 64
TILE = 128
C = 256
DC = 512
FFN = 2048
S_DEV = 8
E_DEV = 1024
CC = 256
GROUPS = 16
HALVES = 2
HC = CC // GROUPS // HALVES
ROWS = HC * 128
eps_norm = 1e-05
bf16 = jnp.bfloat16
f32 = jnp.float32
VMEM_LIMIT = 48 * 1024 * 1024


def dot(a, b):
    return jnp.dot(a, b, preferred_element_type=f32)


def gelu(x):
    inner = 0.7978845608028654 * (x + 0.044715 * (x * x * x))
    return 0.5 * x * (1.0 + jnp.tanh(inner))


def pick_rows(ids_row, width=2 * TILE):
    across = jnp.broadcast_to(ids_row, (TILE, TILE)).astype(f32)
    down = across.T.astype(jnp.int32)
    lanes = lax.broadcasted_iota(jnp.int32, (TILE, TILE), 1)
    parts = [(down == lanes + TILE * i).astype(f32).astype(bf16) for i in range(width // TILE)]
    return jnp.concatenate(parts, axis=1)


def inner_kernel(nbr, x, w1, w2, out, pick, gath):
    first = lax.axis_index("patch") * E_DEV

    @pl.when(pl.program_id(0) == 0)
    def _():
        for j in range(1, 7):
            for k in range(1, 5):
                ids = nbr[k : k + 1, j * TILE : (j + 1) * TILE] - (first + j * TILE - HALO)
                pick[j - 1, (k - 1) * TILE : k * TILE, :] = pick_rows(ids)

    for j in range(1, 7):
        window = x[0, j * TILE - HALO : j * TILE + TILE + HALO, :]
        got = dot(pick[j - 1], window).astype(bf16)
        for k in range(1, 5):
            gath[(j - 1) * TILE : j * TILE, k * C : (k + 1) * C] = got[(k - 1) * TILE : k * TILE]
    centre = x[0, TILE : 7 * TILE, :]
    pre = dot(centre, w1[0:C, :]) + dot(gath[:, C:], w1[C:, :])
    act = gelu(pre).astype(bf16)
    out[0] = (centre.astype(f32) + dot(act, w2[...])).astype(bf16)


def inner(nbr_t, x, w1, w2):
    return pl.pallas_call(
        inner_kernel,
        grid=(S_DEV,),
        in_specs=[
            pl.BlockSpec((5, E_DEV), lambda s: (0, 0)),
            pl.BlockSpec((1, E_DEV, C), lambda s: (s, 0, 0)),
            pl.BlockSpec((5 * C, C), lambda s: (0, 0)),
            pl.BlockSpec((C, C), lambda s: (0, 0)),
        ],
        out_specs=pl.BlockSpec((1, 6 * TILE, C), lambda s: (s, 0, 0)),
        out_shape=jax.ShapeDtypeStruct((S_DEV, 6 * TILE, C), bf16),
        scratch_shapes=[
            pltpu.VMEM((6, 4 * TILE, 2 * TILE), bf16),
            pltpu.VMEM((6 * TILE, 5 * C), bf16),
        ],
        compiler_params=pltpu.CompilerParams(vmem_limit_bytes=VMEM_LIMIT),
        cost_estimate=pl.CostEstimate(flops=8 * 10**9, bytes_accessed=8 * 2**20, transcendentals=2**20),
        name="inner",
    )(nbr_t, x, w1, w2)


SB = 2


def edge_kernel(nbr, own, lo, hi, before, after, mid, w1, w2, edge, send_a, send_b, pick, gath, hot, rec, *sums):
    patch = lax.axis_index("patch")
    step = pl.program_id(0)

    @pl.when(step == 0)
    def _():
        for i, j in enumerate((0, 7)):
            for k in range(1, 5):
                ids = nbr[k : k + 1, j * TILE : (j + 1) * TILE] - (patch * E_DEV + j * TILE - HALO)
                pick[i, (k - 1) * TILE : k * TILE, :] = pick_rows(ids)
        slots = own[...] - patch * CC
        rows = lax.broadcasted_iota(jnp.int32, (CC, E_DEV), 0)
        onehot = (rows == slots).astype(f32)
        hot[...] = onehot.astype(bf16)
        counts = jnp.sum(onehot, axis=1, keepdims=True)
        rec[...] = jnp.broadcast_to(counts, (CC, TILE))

    for s in range(SB):
        low = jnp.concatenate([before[s]] + [lo[s, i] for i in range(3)], axis=0)
        high = jnp.concatenate([hi[s, i] for i in range(1, 4)] + [after[s]], axis=0)
        for i, window in enumerate((low, high)):
            got = dot(pick[i], window).astype(bf16)
            base = (2 * s + i) * TILE
            gath[base : base + TILE, 0:C] = window[HALO : HALO + TILE]
            for k in range(1, 5):
                gath[base : base + TILE, k * C : (k + 1) * C] = got[(k - 1) * TILE : k * TILE]
    act = gelu(dot(gath[...], w1[...])).astype(bf16)
    mixed = (gath[:, 0:C].astype(f32) + dot(act, w2[...])).astype(bf16)
    counts = rec[...]
    counts = jnp.concatenate([counts, counts], axis=1)
    for s in range(SB):
        both = mixed[2 * s * TILE : 2 * (s + 1) * TILE]
        edge[s] = both
        total = dot(hot[:, 0:TILE], both[0:TILE]) + dot(hot[:, 7 * TILE :], both[TILE:])
        total = total + dot(hot[:, TILE : 7 * TILE], mid[s])
        mean = total / counts
        for i in range(2):
            sums[i][pl.ds(step * SB + s, CC, stride=S_DEV), :] = mean[:, i * 128 : (i + 1) * 128]

    @pl.when(step == S_DEV // SB - 1)
    def _():
        block = HC * S_DEV
        for g in range(GROUPS):
            for i in range(2):
                cols = slice(i * 128, (i + 1) * 128)
                send_a[g, :, cols] = sums[i][(2 * g) * block : (2 * g + 1) * block, :].astype(bf16)
                send_b[g, :, cols] = sums[i][(2 * g + 1) * block : (2 * g + 2) * block, :].astype(bf16)


def edges(nbr_t, own, x4, before, after, mid, w1, w2):
    fixed2 = lambda s: (0, 0)
    send = jax.ShapeDtypeStruct((GROUPS, HC * S_DEV, C), bf16)
    return pl.pallas_call(
        edge_kernel,
        grid=(S_DEV // SB,),
        in_specs=[
            pl.BlockSpec((5, E_DEV), fixed2),
            pl.BlockSpec((1, E_DEV), fixed2),
            pl.BlockSpec((SB, 4, HALO, C), lambda s: (s, 0, 0, 0)),
            pl.BlockSpec((SB, 4, HALO, C), lambda s: (s, 3, 0, 0)),
            pl.BlockSpec((SB, HALO, C), lambda s: (s, 0, 0)),
            pl.BlockSpec((SB, HALO, C), lambda s: (s, 0, 0)),
            pl.BlockSpec((SB, 6 * TILE, C), lambda s: (s, 0, 0)),
            pl.BlockSpec((5 * C, C), fixed2),
            pl.BlockSpec((C, C), fixed2),
        ],
        out_specs=[
            pl.BlockSpec((SB, 2 * TILE, C), lambda s: (s, 0, 0)),
            pl.BlockSpec((GROUPS, HC * S_DEV, C), lambda s: (0, 0, 0)),
            pl.BlockSpec((GROUPS, HC * S_DEV, C), lambda s: (0, 0, 0)),
        ],
        out_shape=[jax.ShapeDtypeStruct((S_DEV, 2 * TILE, C), bf16), send, send],
        scratch_shapes=[
            pltpu.VMEM((2, 4 * TILE, 2 * TILE), bf16),
            pltpu.VMEM((SB * 2 * TILE, 5 * C), bf16),
            pltpu.VMEM((CC, E_DEV), bf16),
            pltpu.VMEM((CC, TILE), f32),
            pltpu.VMEM((CC * S_DEV, 128), f32),
            pltpu.VMEM((CC * S_DEV, 128), f32),
        ],
        compiler_params=pltpu.CompilerParams(vmem_limit_bytes=VMEM_LIMIT),
        cost_estimate=pl.CostEstimate(flops=4 * 10**9, bytes_accessed=8 * 2**20, transcendentals=2**19),
        name="edges",
    )(nbr_t, own, x4, x4, before, after, mid, w1, w2)


RB = 512
FB = 512


def rms(rows, gain):
    mean_sq = jnp.mean(rows * rows, axis=-1, keepdims=True)
    return (rows * lax.rsqrt(mean_sq + eps_norm) * gain).astype(bf16)


def layer_kernel(
    x, ga, gf, lift_h, qkv_h, out_h, gate_h, up_h, down_h, dec_h, y,
    lift, wqkv, wout, gate, up, down, dec, flat, qkv, lifted, att, normed, acc, sems,
):
    copies = [
        pltpu.make_async_copy(src, dst, sems.at[i])
        for i, (src, dst) in enumerate(
            (
                (lift_h, lift), (qkv_h, wqkv), (out_h, wout), (gate_h, gate),
                (up_h, up), (down_h, down), (dec_h, dec),
            )
        )
    ]
    for copy in copies:
        copy.start()
    for g in range(GROUPS):
        part = x[g].astype(f32)
        for c in range(HC):
            flat[c * 128 + g * S_DEV : c * 128 + (g + 1) * S_DEV, :] = part[c * S_DEV : (c + 1) * S_DEV]
    lane = lax.broadcasted_iota(jnp.int32, (128, 256), 1) // 64
    causal = lax.broadcasted_iota(jnp.int32, (512, 128), 1) <= (
        lax.broadcasted_iota(jnp.int32, (512, 128), 0) % 128
    )

    def block(b, _):
        r0 = b * RB
        if not isinstance(b, int):
            r0 = pl.multiple_of(r0, RB)

        rows = flat[pl.ds(r0, RB), :].astype(bf16)
        low = dot(rows, lift[...]).astype(bf16)
        lifted[...] = low
        normed[...] = rms(low.astype(f32), ga[...])
        qkv[...] = dot(normed[...], wqkv[...]).astype(bf16)
        for c in range(RB // 128):
            sl = slice(c * 128, (c + 1) * 128)
            for half in range(2):
                q = qkv[sl, half * 256 : half * 256 + 256].astype(f32) * 0.125
                k = qkv[sl, DC + half * 256 : DC + half * 256 + 256]
                v = qkv[sl, 2 * DC + half * 256 : 2 * DC + half * 256 + 256]
                stacked = jnp.concatenate(
                    [jnp.where(lane == h, q, 0.0).astype(bf16) for h in range(4)], axis=0
                )
                scores = lax.dot_general(
                    stacked, k, (((1,), (1,)), ((), ())), preferred_element_type=f32
                )
                scores = jnp.where(causal, scores, -jnp.inf)
                top = jnp.max(scores, axis=-1, keepdims=True)
                e = jnp.exp(scores - top)
                weights = (e / jnp.sum(e, axis=-1, keepdims=True)).astype(bf16)
                full = dot(weights, v)
                o = full[0:128]
                for h in range(1, 4):
                    o = jnp.where(lane == h, full[h * 128 : (h + 1) * 128], o)
                att[sl, half * 256 : half * 256 + 256] = o.astype(bf16)
        one = (lifted[...].astype(f32) + dot(att[...], wout[...])).astype(bf16).astype(f32)
        acc[...] = one
        normed[...] = rms(one, gf[...])
        for n in range(FFN // FB):
            cols = slice(n * FB, (n + 1) * FB)
            g = dot(normed[...], gate[:, cols])
            u = dot(normed[...], up[:, cols])
            hidden = (g * (1.0 / (1.0 + jnp.exp(-g))) * u).astype(bf16)
            acc[...] += dot(hidden, down[cols, :])
        flat[pl.ds(r0, RB), :] = dot(acc[...].astype(bf16), dec[...])
        return 0

    for copy in copies:
        copy.wait()
    lax.fori_loop(0, ROWS // RB, block, 0)
    for g in range(GROUPS):
        y[g] = jnp.concatenate(
            [flat[c * 128 + g * S_DEV : c * 128 + (g + 1) * S_DEV, :] for c in range(HC)], axis=0
        ).astype(bf16)


def layer(x, ga, gf, weights):
    vm = pl.BlockSpec(memory_space=pltpu.VMEM)
    hbm = pl.BlockSpec(memory_space=pl.ANY)
    return pl.pallas_call(
        layer_kernel,
        in_specs=[vm, vm, vm] + [hbm] * 7,
        out_specs=vm,
        out_shape=jax.ShapeDtypeStruct((GROUPS, HC * S_DEV, C), bf16),
        scratch_shapes=[pltpu.VMEM(w.shape, bf16) for w in weights]
        + [
            pltpu.VMEM((ROWS, C), f32),
            pltpu.VMEM((RB, 3 * DC), bf16),
            pltpu.VMEM((RB, DC), bf16),
            pltpu.VMEM((RB, DC), bf16),
            pltpu.VMEM((RB, DC), bf16),
            pltpu.VMEM((RB, DC), f32),
            pltpu.SemaphoreType.DMA((7,)),
        ],
        compiler_params=pltpu.CompilerParams(vmem_limit_bytes=VMEM_LIMIT),
        cost_estimate=pl.CostEstimate(flops=12 * 10**9, bytes_accessed=10 * 2**20, transcendentals=2**22),
        name="layer",
    )(x, ga, gf, *weights)


def spread_kernel(hot, mid, edge, back_a, back_b, out, *flat):
    @pl.when(pl.program_id(0) == 0)
    def _():
        for h in range(2):
            cols = slice(h * 128, (h + 1) * 128)
            flat[h][0:ROWS, :] = back_a[:, cols].astype(f32)
            flat[h][ROWS:, :] = back_b[:, cols].astype(f32)

    for i in range(SB):
        s = pl.program_id(0) * SB + i
        coarse = jnp.concatenate(
            [flat[h][pl.ds(s, CC, stride=S_DEV), :].astype(bf16) for h in range(2)], axis=1
        )
        out[i, 0:TILE, :] = (edge[i, 0:TILE].astype(f32) + dot(hot[0:TILE], coarse)).astype(bf16)
        out[i, TILE : 7 * TILE, :] = (
            mid[i].astype(f32) + dot(hot[TILE : 7 * TILE], coarse)
        ).astype(bf16)
        out[i, 7 * TILE :, :] = (
            edge[i, TILE:].astype(f32) + dot(hot[7 * TILE :], coarse)
        ).astype(bf16)


def spread(hot, mid, edge, back_a, back_b):
    return pl.pallas_call(
        spread_kernel,
        grid=(S_DEV // SB,),
        in_specs=[
            pl.BlockSpec((E_DEV, CC), lambda s: (0, 0)),
            pl.BlockSpec((SB, 6 * TILE, C), lambda s: (s, 0, 0)),
            pl.BlockSpec((SB, 2 * TILE, C), lambda s: (s, 0, 0)),
            pl.BlockSpec((ROWS, C), lambda s: (0, 0)),
            pl.BlockSpec((ROWS, C), lambda s: (0, 0)),
        ],
        out_specs=pl.BlockSpec((SB, E_DEV, C), lambda s: (s, 0, 0)),
        out_shape=jax.ShapeDtypeStruct((S_DEV, E_DEV, C), bf16),
        scratch_shapes=[pltpu.VMEM((2 * ROWS, 128), f32)] * 2,
        compiler_params=pltpu.CompilerParams(vmem_limit_bytes=VMEM_LIMIT),
        cost_estimate=pl.CostEstimate(flops=10**9, bytes_accessed=9 * 2**20, transcendentals=0),
        name="spread",
    )(hot, mid, edge, back_a, back_b)


def exchange(x):
    return lax.all_to_all(x, "tm", split_axis=0, concat_axis=0, tiled=True)


def per_device(
    snapshots, neighbours, owners, w_mix1, w_mix2, w_lift, gain_attn, w_qkv, w_out,
    gain_ffn, w_gate, w_up, w_down, w_dec,
):
    n_patch = lax.axis_size("patch")
    up = [(i, i + 1) for i in range(n_patch - 1)]
    down = [(j, i) for i, j in up]
    before = lax.ppermute(snapshots[:, E_DEV - HALO :], "patch", up)
    after = lax.ppermute(snapshots[:, :HALO], "patch", down)
    nbr_t = neighbours.T
    mid = inner(nbr_t, snapshots, w_mix1, w_mix2)
    x4 = snapshots.reshape(S_DEV, E_DEV // HALO, HALO, C)
    edge, send_a, send_b = edges(
        nbr_t, owners.reshape(1, E_DEV), x4, before, after, mid, w_mix1, w_mix2
    )
    weights = (w_lift, w_qkv, w_out, w_gate, w_up, w_down, w_dec)
    ga, gf = gain_attn.reshape(1, DC), gain_ffn.reshape(1, DC)
    series_a = exchange(send_a)
    series_b = exchange(send_b)
    done_a = layer(series_a, ga, gf, weights)
    back_a = exchange(done_a)
    done_b = layer(series_b, ga, gf, weights)
    back_b = exchange(done_b)
    slots = owners - lax.axis_index("patch") * CC
    group, rest = slots // (2 * HC), slots % (2 * HC)
    place = (rest // HC) * (CC // 2) + group * HC + rest % HC
    hot = (place[:, None] == jnp.arange(CC, dtype=jnp.int32)[None, :]).astype(bf16)
    return spread(
        hot, mid, edge, back_a.reshape(ROWS, C), back_b.reshape(ROWS, C)
    )


def solution(mesh):
    in_specs = (P("tm", "patch", None), P("patch", None), P("patch")) + (P(),) * 11
    return jax.shard_map(
        per_device, mesh=mesh, in_specs=in_specs, out_specs=P("tm", "patch", None), check_vma=False
    )
```

```python
import functools

import jax
import jax.numpy as jnp
from jax import lax
from jax.experimental import pallas as pl
from jax.experimental.pallas import tpu as pltpu
from jax.sharding import PartitionSpec as P

HEADS = 8
HALO = 64
TILE = 128
C = 256
DC = 512
FFN = 2048
S_DEV = 8
E_DEV = 1024
CC = 256
GROUPS = 16
HC = CC // GROUPS
ROWS = HC * 128
eps_norm = 1e-05
bf16 = jnp.bfloat16
f32 = jnp.float32
vm = pl.BlockSpec(memory_space=pltpu.VMEM)
hbm = pl.BlockSpec(memory_space=pltpu.HBM)


def dot(a, b):
    return jnp.dot(a, b, preferred_element_type=f32)


def gelu(x):
    inner = 0.7978845608028654 * (x + 0.044715 * (x * x * x))
    return 0.5 * x * (1.0 + jnp.tanh(inner))


def pick_rows(ids_row, width=2 * TILE):
    across = jnp.broadcast_to(ids_row, (TILE, TILE)).astype(f32)
    down = across.T.astype(jnp.int32)
    lanes = lax.broadcasted_iota(jnp.int32, (TILE, TILE), 1)
    parts = [(down == lanes + TILE * i).astype(f32).astype(bf16) for i in range(width // TILE)]
    return jnp.concatenate(parts, axis=1)


def mix_kernel(
    nbr_h, own_h, x_h, w1_h, w2_h, before, after, mixed_h, send,
    nbr, own, x, w1, w2, mixed, sems, out_sems, pick, gath, hot, counts, *sums,
):
    small = [
        pltpu.make_async_copy(src, dst, sems.at[S_DEV + i])
        for i, (src, dst) in enumerate(((nbr_h, nbr), (own_h, own), (w1_h, w1), (w2_h, w2)))
    ]

    def load(s):
        return pltpu.make_async_copy(x_h.at[s], x.at[s], sems.at[s])

    def save(s):
        return pltpu.make_async_copy(mixed.at[s], mixed_h.at[s], out_sems.at[s])

    for copy in small:
        copy.start()
    for s in range(S_DEV):
        load(s).start()
    small[0].wait()
    small[1].wait()
    patch = lax.axis_index("patch")
    for j in range(8):
        for k in range(1, 5):
            ids = nbr[k : k + 1, j * TILE : (j + 1) * TILE] - (patch * E_DEV + j * TILE - HALO)
            pick[j, (k - 1) * TILE : k * TILE, :] = pick_rows(ids)
    slots = own[...] - patch * CC
    rows = lax.broadcasted_iota(jnp.int32, (CC, E_DEV), 0)
    onehot = (rows == slots).astype(f32)
    hot[...] = onehot.astype(bf16)
    counts[...] = jnp.broadcast_to(jnp.sum(onehot, axis=1, keepdims=True), (CC, TILE))

    small[2].wait()
    small[3].wait()

    def gather(s, base):
        for j in range(8):
            if j == 0:
                window = jnp.concatenate([before[s], x[s, 0 : TILE + HALO]], axis=0)
            elif j == 7:
                window = jnp.concatenate([x[s, E_DEV - TILE - HALO :], after[s]], axis=0)
            else:
                window = x[s, j * TILE - HALO : j * TILE + TILE + HALO]
            got = dot(pick[j], window).astype(bf16)
            to = slice(base + j * TILE, base + (j + 1) * TILE)
            for k in range(4):
                gath[to, k * C : (k + 1) * C] = got[k * TILE : (k + 1) * TILE]

    def snapshots(b, _):
        for i in range(SB):
            load(b * SB + i).wait()
        for i in range(SB):
            gather(b * SB + i, i * E_DEV)
        centre = x[pl.ds(b * SB, SB)].reshape(SB * E_DEV, C)
        pre = dot(centre, w1[0:C, :]) + dot(gath[...], w1[C:, :])
        act = gelu(pre).astype(bf16)
        both = (centre.astype(f32) + dot(act, w2[...])).astype(bf16)
        mixed[pl.ds(b * SB, SB)] = both.reshape(SB, E_DEV, C)
        for i in range(SB):
            save(b * SB + i).start()
        for i in range(SB):
            total = dot(hot[...], both[i * E_DEV : (i + 1) * E_DEV])
            for h in range(2):
                mean = total[:, h * TILE : (h + 1) * TILE] / counts[...]
                sums[h][pl.ds(b * SB + i, CC, stride=S_DEV), :] = mean
        return 0

    lax.fori_loop(0, S_DEV // SB, snapshots, 0)
    for g in range(GROUPS):
        for i in range(2):
            send[g, :, i * TILE : (i + 1) * TILE] = sums[i][
                g * HC * S_DEV : (g + 1) * HC * S_DEV, :
            ].astype(bf16)
    for s in range(S_DEV):
        save(s).wait()


SB = 2


def mix(nbr_t, own, x, before, after, w1, w2):
    return pl.pallas_call(
        mix_kernel,
        in_specs=[hbm] * 5 + [vm] * 2,
        out_specs=[hbm, vm],
        out_shape=[
            pltpu.HBM((S_DEV, E_DEV, C), bf16),
            jax.ShapeDtypeStruct((GROUPS, HC * S_DEV, C), bf16),
        ],
        scratch_shapes=[
            pltpu.VMEM((5, E_DEV), jnp.int32),
            pltpu.VMEM((1, E_DEV), jnp.int32),
            pltpu.VMEM((S_DEV, E_DEV, C), bf16),
            pltpu.VMEM((5 * C, C), bf16),
            pltpu.VMEM((C, C), bf16),
            pltpu.VMEM((S_DEV, E_DEV, C), bf16),
            pltpu.SemaphoreType.DMA((S_DEV + 4,)),
            pltpu.SemaphoreType.DMA((S_DEV,)),
            pltpu.VMEM((8, 4 * TILE, 2 * TILE), bf16),
            pltpu.VMEM((SB * E_DEV, 4 * C), bf16),
            pltpu.VMEM((CC, E_DEV), bf16),
            pltpu.VMEM((CC, TILE), f32),
            pltpu.VMEM((CC * S_DEV, TILE), f32),
            pltpu.VMEM((CC * S_DEV, TILE), f32),
        ],
        compiler_params=pltpu.CompilerParams(vmem_limit_bytes=36 * 2**20),
        cost_estimate=pl.CostEstimate(flops=12 * 10**9, bytes_accessed=2**20, transcendentals=2**21),
        name="mix",
    )(in_hbm(nbr_t), in_hbm(own), in_hbm(x), in_hbm(w1), in_hbm(w2), before, after)


RB = 1024
FB = 256


def rms(rows, gain):
    mean_sq = jnp.mean(rows * rows, axis=-1, keepdims=True)
    return (rows * lax.rsqrt(mean_sq + eps_norm) * gain).astype(bf16)


def layer_kernel(
    x, ga, gf, lift, wqkv, wout, gate, up, down, dec, y,
    flat, qkv, lifted, att, normed, acc, hidden,
):
    for g in range(GROUPS):
        part = x[g].astype(f32)
        for c in range(HC):
            flat[c * 128 + g * S_DEV : c * 128 + (g + 1) * S_DEV, :] = part[c * S_DEV : (c + 1) * S_DEV]
    lane = lax.broadcasted_iota(jnp.int32, (128, 256), 1) // 64
    causal = lax.broadcasted_iota(jnp.int32, (512, 128), 1) <= (
        lax.broadcasted_iota(jnp.int32, (512, 128), 0) % 128
    )

    def block(b, _):
        r0 = b * RB
        if not isinstance(b, int):
            r0 = pl.multiple_of(r0, RB)

        rows = flat[pl.ds(r0, RB), :].astype(bf16)
        low = dot(rows, lift[...]).astype(bf16)
        lifted[...] = low
        normed[...] = rms(low.astype(f32), ga[...])
        qkv[...] = dot(normed[...], wqkv[...]).astype(bf16)
        for c in range(RB // 128):
            sl = slice(c * 128, (c + 1) * 128)
            for half in range(2):
                q = qkv[sl, half * 256 : half * 256 + 256].astype(f32) * 0.125
                k = qkv[sl, DC + half * 256 : DC + half * 256 + 256]
                v = qkv[sl, 2 * DC + half * 256 : 2 * DC + half * 256 + 256]
                stacked = jnp.concatenate(
                    [jnp.where(lane == h, q, 0.0).astype(bf16) for h in range(4)], axis=0
                )
                scores = lax.dot_general(
                    stacked, k, (((1,), (1,)), ((), ())), preferred_element_type=f32
                )
                scores = jnp.where(causal, scores, -jnp.inf)
                top = jnp.max(scores, axis=-1, keepdims=True)
                e = jnp.exp(scores - top)
                share = 1.0 / jnp.sum(e, axis=-1, keepdims=True)
                full = dot(e.astype(bf16), v) * share
                o = full[0:128]
                for h in range(1, 4):
                    o = jnp.where(lane == h, full[h * 128 : (h + 1) * 128], o)
                att[sl, half * 256 : half * 256 + 256] = o.astype(bf16)
        one = (lifted[...].astype(f32) + dot(att[...], wout[...])).astype(bf16).astype(f32)
        acc[...] = one
        normed[...] = rms(one, gf[...])
        for n in range(FFN // FB):
            cols = slice(n * FB, (n + 1) * FB)
            g = dot(normed[...], gate[:, cols])
            u = dot(normed[...], up[:, cols])
            hidden[:, cols] = (g * (1.0 / (1.0 + jnp.exp(-g))) * u).astype(bf16)
        two = (acc[...] + dot(hidden[...], down[...])).astype(bf16)
        flat[pl.ds(r0, RB), :] = dot(two, dec[...])
        return 0

    lax.fori_loop(0, ROWS // RB, block, 0)
    for g in range(GROUPS):
        y[g] = jnp.concatenate(
            [flat[c * 128 + g * S_DEV : c * 128 + (g + 1) * S_DEV, :] for c in range(HC)], axis=0
        ).astype(bf16)


def layer(x, ga, gf, weights):
    return pl.pallas_call(
        layer_kernel,
        in_specs=[vm] * 10,
        out_specs=vm,
        out_shape=jax.ShapeDtypeStruct((GROUPS, HC * S_DEV, C), bf16),
        scratch_shapes=[
            pltpu.VMEM((ROWS, C), f32),
            pltpu.VMEM((RB, 3 * DC), bf16),
            pltpu.VMEM((RB, DC), bf16),
            pltpu.VMEM((RB, DC), bf16),
            pltpu.VMEM((RB, DC), bf16),
            pltpu.VMEM((RB, DC), f32),
            pltpu.VMEM((RB, FFN), bf16),
        ],
        compiler_params=pltpu.CompilerParams(vmem_limit_bytes=32 * 2**20),
        cost_estimate=pl.CostEstimate(flops=24 * 10**9, bytes_accessed=2**20, transcendentals=2**22),
        name="layer",
    )(x, ga, gf, *weights)


def spread_kernel(mixed_h, hot, back, out_h, stage, in_sems, out_sems, *flat):
    def load(s):
        return pltpu.make_async_copy(mixed_h.at[s], stage.at[s], in_sems.at[s])

    def save(s):
        return pltpu.make_async_copy(stage.at[s], out_h.at[s], out_sems.at[s])

    for s in range(S_DEV):
        load(s).start()
    for h in range(2):
        flat[h][...] = back[:, h * TILE : (h + 1) * TILE].astype(f32)
    for s in range(S_DEV):
        coarse = jnp.concatenate(
            [flat[h][pl.ds(s, CC, stride=S_DEV), :].astype(bf16) for h in range(2)], axis=1
        )
        load(s).wait()
        stage[s] = (stage[s].astype(f32) + dot(hot[...], coarse)).astype(bf16)
        save(s).start()
    for s in range(S_DEV):
        save(s).wait()


def spread(mixed, hot, back):
    return pl.pallas_call(
        spread_kernel,
        in_specs=[hbm, vm, vm],
        out_specs=hbm,
        out_shape=jax.ShapeDtypeStruct((S_DEV, E_DEV, C), bf16),
        scratch_shapes=[
            pltpu.VMEM((S_DEV, E_DEV, C), bf16),
            pltpu.SemaphoreType.DMA((S_DEV,)),
            pltpu.SemaphoreType.DMA((S_DEV,)),
            pltpu.VMEM((ROWS, TILE), f32),
            pltpu.VMEM((ROWS, TILE), f32),
        ],
        compiler_params=pltpu.CompilerParams(vmem_limit_bytes=24 * 2**20),
        cost_estimate=pl.CostEstimate(flops=10**9, bytes_accessed=8 * 2**20, transcendentals=0),
        name="spread",
    )(in_hbm(mixed), hot, back)


def in_hbm(array):
    return pltpu.with_memory_space_constraint(array, pltpu.HBM)


def exchange(x):
    return lax.all_to_all(x, "tm", split_axis=0, concat_axis=0, tiled=True)


def per_device(
    snapshots, neighbours, owners, w_mix1, w_mix2, w_lift, gain_attn, w_qkv, w_out,
    gain_ffn, w_gate, w_up, w_down, w_dec,
):
    n_patch = lax.axis_size("patch")
    up = [(i, i + 1) for i in range(n_patch - 1)]
    down = [(j, i) for i, j in up]
    before = lax.ppermute(snapshots[:, E_DEV - HALO :], "patch", up)
    after = lax.ppermute(snapshots[:, :HALO], "patch", down)
    nbr_t = neighbours.T
    mixed, send = mix(
        nbr_t, owners.reshape(1, E_DEV), snapshots, before, after, w_mix1, w_mix2
    )
    weights = (w_lift, w_qkv, w_out, w_gate, w_up, w_down, w_dec)
    ga, gf = gain_attn.reshape(1, DC), gain_ffn.reshape(1, DC)
    back = exchange(layer(exchange(send), ga, gf, weights))
    slots = owners - lax.axis_index("patch") * CC
    hot = (slots[:, None] == jnp.arange(CC, dtype=jnp.int32)[None, :]).astype(bf16)
    return spread(mixed, hot, back.reshape(ROWS, C))


def solution(mesh):
    in_specs = (P("tm", "patch", None), P("patch", None), P("patch")) + (P(),) * 11
    return jax.shard_map(
        per_device, mesh=mesh, in_specs=in_specs, out_specs=P("tm", "patch", None), check_vma=False
    )
```

```python
import functools

import jax
import jax.numpy as jnp
from jax import lax
from jax.experimental import pallas as pl
from jax.experimental.pallas import tpu as pltpu
from jax.sharding import PartitionSpec as P

HEADS = 8
HALO = 64
TILE = 128
C = 256
DC = 512
FFN = 2048
S_DEV = 8
E_DEV = 1024
CC = 256
GROUPS = 16
HC = CC // GROUPS
ROWS = HC * 128
eps_norm = 1e-05
bf16 = jnp.bfloat16
f32 = jnp.float32
vm = pl.BlockSpec(memory_space=pltpu.VMEM)
hbm = pl.BlockSpec(memory_space=pltpu.HBM)


def dot(a, b):
    return jnp.dot(a, b, preferred_element_type=f32)


def gelu(x):
    inner = 0.7978845608028654 * (x + 0.044715 * (x * x * x))
    return 0.5 * x * (1.0 + jnp.tanh(inner))


def pick_rows(ids_row, width=2 * TILE):
    across = jnp.broadcast_to(ids_row, (TILE, TILE)).astype(f32)
    down = across.T.astype(jnp.int32)
    lanes = lax.broadcasted_iota(jnp.int32, (TILE, TILE), 1)
    parts = [(down == lanes + TILE * i).astype(f32).astype(bf16) for i in range(width // TILE)]
    return jnp.concatenate(parts, axis=1)


def mix_kernel(
    nbr_h, own_h, x_h, w1_h, w2_h, before, after, mixed, send, unpool,
    nbr, own, x, w1, w2, sems, pick, gath, hot, share, *sums,
):
    small = [
        pltpu.make_async_copy(src, dst, sems.at[S_DEV + i])
        for i, (src, dst) in enumerate(((nbr_h, nbr), (own_h, own), (w1_h, w1), (w2_h, w2)))
    ]

    def load(s):
        return pltpu.make_async_copy(x_h.at[s], x.at[s], sems.at[s])

    for copy in small:
        copy.start()
    for s in range(S_DEV):
        load(s).start()
    small[0].wait()
    small[1].wait()
    patch = lax.axis_index("patch")
    for j in range(8):
        for k in range(1, 5):
            ids = nbr[k : k + 1, j * TILE : (j + 1) * TILE] - (patch * E_DEV + j * TILE - HALO)
            pick[j, (k - 1) * TILE : k * TILE, :] = pick_rows(ids)
    slots = own[...] - patch * CC
    for j in range(8):
        unpool[j * TILE : (j + 1) * TILE, :] = pick_rows(slots[:, j * TILE : (j + 1) * TILE])
    rows = lax.broadcasted_iota(jnp.int32, (CC, E_DEV), 0)
    onehot = (rows == slots).astype(f32)
    hot[...] = onehot.astype(bf16)
    share[...] = jnp.broadcast_to(1.0 / jnp.sum(onehot, axis=1, keepdims=True), (CC, TILE))

    small[2].wait()
    small[3].wait()

    def gather(s, base):
        for j in range(8):
            if j == 0:
                window = jnp.concatenate([before[s], x[s, 0 : TILE + HALO]], axis=0)
            elif j == 7:
                window = jnp.concatenate([x[s, E_DEV - TILE - HALO :], after[s]], axis=0)
            else:
                window = x[s, j * TILE - HALO : j * TILE + TILE + HALO]
            got = dot(pick[j], window).astype(bf16)
            to = slice(base + j * TILE, base + (j + 1) * TILE)
            for k in range(4):
                gath[to, k * C : (k + 1) * C] = got[k * TILE : (k + 1) * TILE]

    def snapshots(b, _):
        for i in range(SB):
            load(b * SB + i).wait()
        for i in range(SB):
            gather(b * SB + i, i * E_DEV)
        centre = x[pl.ds(b * SB, SB)].reshape(SB * E_DEV, C)
        pre = dot(centre, w1[0:C, :]) + dot(gath[...], w1[C:, :])
        act = gelu(pre).astype(bf16)
        both = (centre.astype(f32) + dot(act, w2[...])).astype(bf16)
        mixed[pl.ds(b * SB, SB)] = both.reshape(SB, E_DEV, C)
        for i in range(SB):
            total = dot(hot[...], both[i * E_DEV : (i + 1) * E_DEV])
            for h in range(2):
                mean = total[:, h * TILE : (h + 1) * TILE] * share[...]
                sums[h][pl.ds(b * SB + i, CC, stride=S_DEV), :] = mean
        return 0

    lax.fori_loop(0, S_DEV // SB, snapshots, 0)
    for g in range(GROUPS):
        for i in range(2):
            send[g, :, i * TILE : (i + 1) * TILE] = sums[i][
                g * HC * S_DEV : (g + 1) * HC * S_DEV, :
            ].astype(bf16)


SB = 2


def mix(nbr_t, own, x, before, after, w1, w2):
    return pl.pallas_call(
        mix_kernel,
        in_specs=[hbm] * 5 + [vm] * 2,
        out_specs=[vm] * 3,
        out_shape=[
            jax.ShapeDtypeStruct((S_DEV, E_DEV, C), bf16),
            jax.ShapeDtypeStruct((GROUPS, HC * S_DEV, C), bf16),
            jax.ShapeDtypeStruct((E_DEV, CC), bf16),
        ],
        scratch_shapes=[
            pltpu.VMEM((5, E_DEV), jnp.int32),
            pltpu.VMEM((1, E_DEV), jnp.int32),
            pltpu.VMEM((S_DEV, E_DEV, C), bf16),
            pltpu.VMEM((5 * C, C), bf16),
            pltpu.VMEM((C, C), bf16),
            pltpu.SemaphoreType.DMA((S_DEV + 4,)),
            pltpu.VMEM((8, 4 * TILE, 2 * TILE), bf16),
            pltpu.VMEM((SB * E_DEV, 4 * C), bf16),
            pltpu.VMEM((CC, E_DEV), bf16),
            pltpu.VMEM((CC, TILE), f32),
            pltpu.VMEM((CC * S_DEV, TILE), f32),
            pltpu.VMEM((CC * S_DEV, TILE), f32),
        ],
        compiler_params=pltpu.CompilerParams(vmem_limit_bytes=32 * 2**20),
        cost_estimate=pl.CostEstimate(flops=12 * 10**9, bytes_accessed=2**20, transcendentals=2**21),
        name="mix",
    )(in_hbm(nbr_t), in_hbm(own), in_hbm(x), in_hbm(w1), in_hbm(w2), before, after)


RB = 1024
FB = 256


def rms(rows, gain):
    mean_sq = jnp.mean(rows * rows, axis=-1, keepdims=True)
    return (rows * lax.rsqrt(mean_sq + eps_norm) * gain).astype(bf16)


def layer_kernel(
    x, ga, gf, lift, wqkv, wout, gate, up, down, dec, y,
    flat, qkv, lifted, att, normed, acc, hidden,
):
    for g in range(GROUPS):
        part = x[g].astype(f32)
        for c in range(HC):
            flat[c * 128 + g * S_DEV : c * 128 + (g + 1) * S_DEV, :] = part[c * S_DEV : (c + 1) * S_DEV]
    lane = lax.broadcasted_iota(jnp.int32, (128, 256), 1) // 64
    causal = lax.broadcasted_iota(jnp.int32, (512, 128), 1) <= (
        lax.broadcasted_iota(jnp.int32, (512, 128), 0) % 128
    )

    def block(b, _):
        r0 = b * RB
        if not isinstance(b, int):
            r0 = pl.multiple_of(r0, RB)

        rows = flat[pl.ds(r0, RB), :].astype(bf16)
        low = dot(rows, lift[...]).astype(bf16)
        lifted[...] = low
        normed[...] = rms(low.astype(f32), ga[...])
        qkv[...] = dot(normed[...], wqkv[...]).astype(bf16)
        for c in range(RB // 128):
            sl = slice(c * 128, (c + 1) * 128)
            for half in range(2):
                q = qkv[sl, half * 256 : half * 256 + 256].astype(f32) * 0.125
                k = qkv[sl, DC + half * 256 : DC + half * 256 + 256]
                v = qkv[sl, 2 * DC + half * 256 : 2 * DC + half * 256 + 256]
                stacked = jnp.concatenate(
                    [jnp.where(lane == h, q, 0.0).astype(bf16) for h in range(4)], axis=0
                )
                scores = lax.dot_general(
                    stacked, k, (((1,), (1,)), ((), ())), preferred_element_type=f32
                )
                scores = jnp.where(causal, scores, -jnp.inf)
                top = jnp.max(scores, axis=-1, keepdims=True)
                e = jnp.exp(scores - top)
                share = 1.0 / jnp.sum(e, axis=-1, keepdims=True)
                full = dot(e.astype(bf16), v) * share
                o = full[0:128]
                for h in range(1, 4):
                    o = jnp.where(lane == h, full[h * 128 : (h + 1) * 128], o)
                att[sl, half * 256 : half * 256 + 256] = o.astype(bf16)
        one = (lifted[...].astype(f32) + dot(att[...], wout[...])).astype(bf16).astype(f32)
        acc[...] = one
        normed[...] = rms(one, gf[...])
        for n in range(FFN // FB):
            cols = slice(n * FB, (n + 1) * FB)
            g = dot(normed[...], gate[:, cols])
            u = dot(normed[...], up[:, cols])
            hidden[:, cols] = (g * (1.0 / (1.0 + jnp.exp(-g))) * u).astype(bf16)
        two = (acc[...] + dot(hidden[...], down[...])).astype(bf16)
        flat[pl.ds(r0, RB), :] = dot(two, dec[...])
        return 0

    lax.fori_loop(0, ROWS // RB, block, 0)
    for g in range(GROUPS):
        y[g] = jnp.concatenate(
            [flat[c * 128 + g * S_DEV : c * 128 + (g + 1) * S_DEV, :] for c in range(HC)], axis=0
        ).astype(bf16)


def layer(x, ga, gf, weights):
    return pl.pallas_call(
        layer_kernel,
        in_specs=[vm] * 10,
        out_specs=vm,
        out_shape=jax.ShapeDtypeStruct((GROUPS, HC * S_DEV, C), bf16),
        scratch_shapes=[
            pltpu.VMEM((ROWS, C), f32),
            pltpu.VMEM((RB, 3 * DC), bf16),
            pltpu.VMEM((RB, DC), bf16),
            pltpu.VMEM((RB, DC), bf16),
            pltpu.VMEM((RB, DC), bf16),
            pltpu.VMEM((RB, DC), f32),
            pltpu.VMEM((RB, FFN), bf16),
        ],
        compiler_params=pltpu.CompilerParams(vmem_limit_bytes=32 * 2**20),
        cost_estimate=pl.CostEstimate(flops=24 * 10**9, bytes_accessed=2**20, transcendentals=2**22),
        name="layer",
    )(x, ga, gf, *weights)


def spread_kernel(mixed, hot, back, out_h, stage, out_sems, *flat):
    def save(s):
        return pltpu.make_async_copy(stage.at[s], out_h.at[s], out_sems.at[s])

    for h in range(2):
        flat[h][...] = back[:, h * TILE : (h + 1) * TILE].astype(f32)
    for s in range(S_DEV):
        coarse = jnp.concatenate(
            [flat[h][pl.ds(s, CC, stride=S_DEV), :].astype(bf16) for h in range(2)], axis=1
        )
        stage[s] = (mixed[s].astype(f32) + dot(hot[...], coarse)).astype(bf16)
        save(s).start()
    for s in range(S_DEV):
        save(s).wait()


def spread(mixed, hot, back):
    return pl.pallas_call(
        spread_kernel,
        in_specs=[vm, vm, vm],
        out_specs=hbm,
        out_shape=jax.ShapeDtypeStruct((S_DEV, E_DEV, C), bf16),
        scratch_shapes=[
            pltpu.VMEM((S_DEV, E_DEV, C), bf16),
            pltpu.SemaphoreType.DMA((S_DEV,)),
            pltpu.VMEM((ROWS, TILE), f32),
            pltpu.VMEM((ROWS, TILE), f32),
        ],
        compiler_params=pltpu.CompilerParams(vmem_limit_bytes=24 * 2**20),
        cost_estimate=pl.CostEstimate(flops=10**9, bytes_accessed=8 * 2**20, transcendentals=0),
        name="spread",
    )(mixed, hot, back)


def in_hbm(array):
    return pltpu.with_memory_space_constraint(array, pltpu.HBM)


def exchange(x):
    return lax.all_to_all(x, "tm", split_axis=0, concat_axis=0, tiled=True)


def per_device(
    snapshots, neighbours, owners, w_mix1, w_mix2, w_lift, gain_attn, w_qkv, w_out,
    gain_ffn, w_gate, w_up, w_down, w_dec,
):
    n_patch = lax.axis_size("patch")
    up = [(i, i + 1) for i in range(n_patch - 1)]
    down = [(j, i) for i, j in up]
    before = lax.ppermute(snapshots[:, E_DEV - HALO :], "patch", up)
    after = lax.ppermute(snapshots[:, :HALO], "patch", down)
    nbr_t = neighbours.T
    mixed, send, hot = mix(
        nbr_t, owners.reshape(1, E_DEV), snapshots, before, after, w_mix1, w_mix2
    )
    weights = (w_lift, w_qkv, w_out, w_gate, w_up, w_down, w_dec)
    ga, gf = gain_attn.reshape(1, DC), gain_ffn.reshape(1, DC)
    back = exchange(layer(exchange(send), ga, gf, weights))
    return spread(mixed, hot, back.reshape(ROWS, C))


def solution(mesh):
    in_specs = (P("tm", "patch", None), P("patch", None), P("patch")) + (P(),) * 11
    return jax.shard_map(
        per_device, mesh=mesh, in_specs=in_specs, out_specs=P("tm", "patch", None), check_vma=False
    )
```

```python
import functools

import jax
import jax.numpy as jnp
from jax import lax
from jax.experimental import pallas as pl
from jax.experimental.pallas import tpu as pltpu
from jax.sharding import PartitionSpec as P

HEADS = 8
HALO = 64
TILE = 128
C = 256
DC = 512
FFN = 2048
S_DEV = 8
E_DEV = 1024
CC = 256
GROUPS = 16
HC = CC // GROUPS
ROWS = HC * 128
eps_norm = 1e-05
bf16 = jnp.bfloat16
f32 = jnp.float32
vm = pl.BlockSpec(memory_space=pltpu.VMEM)
hbm = pl.BlockSpec(memory_space=pltpu.HBM)


def dot(a, b):
    return jnp.dot(a, b, preferred_element_type=f32)


def gelu(x):
    inner = 0.7978845608028654 * (x + 0.044715 * (x * x * x))
    return 0.5 * x * (1.0 + jnp.tanh(inner))


def pick_rows(ids_row, width=2 * TILE):
    across = jnp.broadcast_to(ids_row, (TILE, TILE)).astype(f32)
    down = across.T.astype(jnp.int32)
    lanes = lax.broadcasted_iota(jnp.int32, (TILE, TILE), 1)
    parts = [(down == lanes + TILE * i).astype(f32).astype(bf16) for i in range(width // TILE)]
    return jnp.concatenate(parts, axis=1)


def prepare_kernel(
    nbr_h, own_h, x_h, w1_h, w2_h, x, w1, w2, pick, hot, unpool, share, nbr, own, sems
):
    pairs = ((nbr_h, nbr), (own_h, own), (w1_h, w1), (w2_h, w2)) + tuple(
        (x_h.at[s], x.at[s]) for s in range(S_DEV)
    )
    copies = [pltpu.make_async_copy(src, dst, sems.at[i]) for i, (src, dst) in enumerate(pairs)]
    for copy in copies:
        copy.start()
    copies[0].wait()
    copies[1].wait()
    patch = lax.axis_index("patch")
    for j in range(8):
        for k in range(1, 5):
            ids = nbr[k : k + 1, j * TILE : (j + 1) * TILE] - (patch * E_DEV + j * TILE - HALO)
            pick[j, (k - 1) * TILE : k * TILE, :] = pick_rows(ids)
    slots = own[...] - patch * CC
    for j in range(8):
        unpool[j * TILE : (j + 1) * TILE, :] = pick_rows(slots[:, j * TILE : (j + 1) * TILE])
    rows = lax.broadcasted_iota(jnp.int32, (CC, E_DEV), 0)
    onehot = (rows == slots).astype(f32)
    hot[...] = onehot.astype(bf16)
    share[...] = jnp.broadcast_to(1.0 / jnp.sum(onehot, axis=1, keepdims=True), (CC, TILE))
    for copy in copies[2:]:
        copy.wait()


def prepare(nbr_t, own, x, w1, w2):
    return pl.pallas_call(
        prepare_kernel,
        in_specs=[hbm] * 5,
        out_specs=[vm] * 7,
        out_shape=[
            pltpu.VMEM((S_DEV, E_DEV, C), bf16),
            pltpu.VMEM((5 * C, C), bf16),
            pltpu.VMEM((C, C), bf16),
            pltpu.VMEM((8, 4 * TILE, 2 * TILE), bf16),
            pltpu.VMEM((CC, E_DEV), bf16),
            jax.ShapeDtypeStruct((E_DEV, CC), bf16),
            pltpu.VMEM((CC, TILE), f32),
        ],
        scratch_shapes=[
            pltpu.VMEM((5, E_DEV), jnp.int32),
            pltpu.VMEM((1, E_DEV), jnp.int32),
            pltpu.SemaphoreType.DMA((S_DEV + 4,)),
        ],
        compiler_params=pltpu.CompilerParams(vmem_limit_bytes=16 * 2**20),
        cost_estimate=pl.CostEstimate(flops=10**9, bytes_accessed=5 * 2**20, transcendentals=0),
        name="prepare",
    )(in_hbm(nbr_t), in_hbm(own), in_hbm(x), in_hbm(w1), in_hbm(w2))


def mix_kernel(x, w1, w2, pick, hot, share, before, after, mixed, send, gath, *sums):
    def gather(s, base):
        for j in range(8):
            if j == 0:
                window = jnp.concatenate([before[s], x[s, 0 : TILE + HALO]], axis=0)
            elif j == 7:
                window = jnp.concatenate([x[s, E_DEV - TILE - HALO :], after[s]], axis=0)
            else:
                window = x[s, j * TILE - HALO : j * TILE + TILE + HALO]
            got = dot(pick[j], window).astype(bf16)
            to = slice(base + j * TILE, base + (j + 1) * TILE)
            for k in range(4):
                gath[to, k * C : (k + 1) * C] = got[k * TILE : (k + 1) * TILE]

    def snapshots(b, _):
        for i in range(SB):
            gather(b * SB + i, i * E_DEV)
        centre = x[pl.ds(b * SB, SB)].reshape(SB * E_DEV, C)
        pre = dot(centre, w1[0:C, :]) + dot(gath[...], w1[C:, :])
        act = gelu(pre).astype(bf16)
        both = (centre.astype(f32) + dot(act, w2[...])).astype(bf16)
        mixed[pl.ds(b * SB, SB)] = both.reshape(SB, E_DEV, C)
        for i in range(SB):
            total = dot(hot[...], both[i * E_DEV : (i + 1) * E_DEV])
            for h in range(2):
                mean = total[:, h * TILE : (h + 1) * TILE] * share[...]
                sums[h][pl.ds(b * SB + i, CC, stride=S_DEV), :] = mean
        return 0

    lax.fori_loop(0, S_DEV // SB, snapshots, 0)
    for g in range(GROUPS):
        for i in range(2):
            send[g, :, i * TILE : (i + 1) * TILE] = sums[i][
                g * HC * S_DEV : (g + 1) * HC * S_DEV, :
            ].astype(bf16)


SB = 2


def mix(x, w1, w2, pick, hot, share, before, after):
    return pl.pallas_call(
        mix_kernel,
        in_specs=[vm] * 8,
        out_specs=[vm] * 2,
        out_shape=[
            jax.ShapeDtypeStruct((S_DEV, E_DEV, C), bf16),
            jax.ShapeDtypeStruct((GROUPS, HC * S_DEV, C), bf16),
        ],
        scratch_shapes=[
            pltpu.VMEM((SB * E_DEV, 4 * C), bf16),
            pltpu.VMEM((CC * S_DEV, TILE), f32),
            pltpu.VMEM((CC * S_DEV, TILE), f32),
        ],
        compiler_params=pltpu.CompilerParams(vmem_limit_bytes=26 * 2**20),
        cost_estimate=pl.CostEstimate(flops=12 * 10**9, bytes_accessed=2**20, transcendentals=2**21),
        name="mix",
    )(x, w1, w2, pick, hot, share, before, after)


RB = 1024
FB = 256


def rms(rows, gain):
    mean_sq = jnp.mean(rows * rows, axis=-1, keepdims=True)
    return (rows * lax.rsqrt(mean_sq + eps_norm) * gain).astype(bf16)


def layer_kernel(
    x, ga, gf, lift, wqkv, wout, gate, up, down, dec, y,
    flat, qkv, lifted, att, normed, acc, hidden,
):
    for g in range(GROUPS):
        part = x[g].astype(f32)
        for c in range(HC):
            flat[c * 128 + g * S_DEV : c * 128 + (g + 1) * S_DEV, :] = part[c * S_DEV : (c + 1) * S_DEV]
    lane = lax.broadcasted_iota(jnp.int32, (128, 256), 1) // 64
    causal = lax.broadcasted_iota(jnp.int32, (512, 128), 1) <= (
        lax.broadcasted_iota(jnp.int32, (512, 128), 0) % 128
    )

    def block(b, _):
        r0 = b * RB
        if not isinstance(b, int):
            r0 = pl.multiple_of(r0, RB)

        rows = flat[pl.ds(r0, RB), :].astype(bf16)
        low = dot(rows, lift[...]).astype(bf16)
        lifted[...] = low
        normed[...] = rms(low.astype(f32), ga[...])
        qkv[...] = dot(normed[...], wqkv[...]).astype(bf16)
        for c in range(RB // 128):
            sl = slice(c * 128, (c + 1) * 128)
            for half in range(2):
                q = qkv[sl, half * 256 : half * 256 + 256].astype(f32) * 0.125
                k = qkv[sl, DC + half * 256 : DC + half * 256 + 256]
                v = qkv[sl, 2 * DC + half * 256 : 2 * DC + half * 256 + 256]
                stacked = jnp.concatenate(
                    [jnp.where(lane == h, q, 0.0).astype(bf16) for h in range(4)], axis=0
                )
                scores = lax.dot_general(
                    stacked, k, (((1,), (1,)), ((), ())), preferred_element_type=f32
                )
                scores = jnp.where(causal, scores, -jnp.inf)
                top = jnp.max(scores, axis=-1, keepdims=True)
                e = jnp.exp(scores - top)
                share = 1.0 / jnp.sum(e, axis=-1, keepdims=True)
                full = dot(e.astype(bf16), v) * share
                o = full[0:128]
                for h in range(1, 4):
                    o = jnp.where(lane == h, full[h * 128 : (h + 1) * 128], o)
                att[sl, half * 256 : half * 256 + 256] = o.astype(bf16)
        one = (lifted[...].astype(f32) + dot(att[...], wout[...])).astype(bf16).astype(f32)
        acc[...] = one
        normed[...] = rms(one, gf[...])
        for n in range(FFN // FB):
            cols = slice(n * FB, (n + 1) * FB)
            g = dot(normed[...], gate[:, cols])
            u = dot(normed[...], up[:, cols])
            hidden[:, cols] = (g * (1.0 / (1.0 + jnp.exp(-g))) * u).astype(bf16)
        two = (acc[...] + dot(hidden[...], down[...])).astype(bf16)
        flat[pl.ds(r0, RB), :] = dot(two, dec[...])
        return 0

    lax.fori_loop(0, ROWS // RB, block, 0)
    for g in range(GROUPS):
        y[g] = jnp.concatenate(
            [flat[c * 128 + g * S_DEV : c * 128 + (g + 1) * S_DEV, :] for c in range(HC)], axis=0
        ).astype(bf16)


def layer(x, ga, gf, weights):
    return pl.pallas_call(
        layer_kernel,
        in_specs=[vm] * 10,
        out_specs=vm,
        out_shape=jax.ShapeDtypeStruct((GROUPS, HC * S_DEV, C), bf16),
        scratch_shapes=[
            pltpu.VMEM((ROWS, C), f32),
            pltpu.VMEM((RB, 3 * DC), bf16),
            pltpu.VMEM((RB, DC), bf16),
            pltpu.VMEM((RB, DC), bf16),
            pltpu.VMEM((RB, DC), bf16),
            pltpu.VMEM((RB, DC), f32),
            pltpu.VMEM((RB, FFN), bf16),
        ],
        compiler_params=pltpu.CompilerParams(vmem_limit_bytes=32 * 2**20),
        cost_estimate=pl.CostEstimate(flops=24 * 10**9, bytes_accessed=2**20, transcendentals=2**22),
        name="layer",
    )(x, ga, gf, *weights)


def spread_kernel(mixed, hot, back, out_h, stage, out_sems, *flat):
    def save(s):
        return pltpu.make_async_copy(stage.at[s], out_h.at[s], out_sems.at[s])

    for h in range(2):
        flat[h][...] = back[:, h * TILE : (h + 1) * TILE].astype(f32)
    for s in range(S_DEV):
        coarse = jnp.concatenate(
            [flat[h][pl.ds(s, CC, stride=S_DEV), :].astype(bf16) for h in range(2)], axis=1
        )
        stage[s] = (mixed[s].astype(f32) + dot(hot[...], coarse)).astype(bf16)
        save(s).start()
    for s in range(S_DEV):
        save(s).wait()


def spread(mixed, hot, back):
    return pl.pallas_call(
        spread_kernel,
        in_specs=[vm, vm, vm],
        out_specs=hbm,
        out_shape=jax.ShapeDtypeStruct((S_DEV, E_DEV, C), bf16),
        scratch_shapes=[
            pltpu.VMEM((S_DEV, E_DEV, C), bf16),
            pltpu.SemaphoreType.DMA((S_DEV,)),
            pltpu.VMEM((ROWS, TILE), f32),
            pltpu.VMEM((ROWS, TILE), f32),
        ],
        compiler_params=pltpu.CompilerParams(vmem_limit_bytes=24 * 2**20),
        cost_estimate=pl.CostEstimate(flops=10**9, bytes_accessed=8 * 2**20, transcendentals=0),
        name="spread",
    )(mixed, hot, back)


def in_hbm(array):
    return pltpu.with_memory_space_constraint(array, pltpu.HBM)


def exchange(x):
    return lax.all_to_all(x, "tm", split_axis=0, concat_axis=0, tiled=True)


def per_device(
    snapshots, neighbours, owners, w_mix1, w_mix2, w_lift, gain_attn, w_qkv, w_out,
    gain_ffn, w_gate, w_up, w_down, w_dec,
):
    n_patch = lax.axis_size("patch")
    up = [(i, i + 1) for i in range(n_patch - 1)]
    down = [(j, i) for i, j in up]
    before = lax.ppermute(snapshots[:, E_DEV - HALO :], "patch", up)
    after = lax.ppermute(snapshots[:, :HALO], "patch", down)
    nbr_t = neighbours.T
    x, w1, w2, pick, hot, unpool, share = prepare(
        nbr_t, owners.reshape(1, E_DEV), snapshots, w_mix1, w_mix2
    )
    mixed, send = mix(x, w1, w2, pick, hot, share, before, after)
    weights = (w_lift, w_qkv, w_out, w_gate, w_up, w_down, w_dec)
    ga, gf = gain_attn.reshape(1, DC), gain_ffn.reshape(1, DC)
    back = exchange(layer(exchange(send), ga, gf, weights))
    return spread(mixed, unpool, back.reshape(ROWS, C))


def solution(mesh):
    in_specs = (P("tm", "patch", None), P("patch", None), P("patch")) + (P(),) * 11
    return jax.shard_map(
        per_device, mesh=mesh, in_specs=in_specs, out_specs=P("tm", "patch", None), check_vma=False
    )
```

```python
import functools

import jax
import jax.numpy as jnp
from jax import lax
from jax.experimental import pallas as pl
from jax.experimental.pallas import tpu as pltpu
from jax.sharding import PartitionSpec as P

HEADS = 8
HALO = 64
TILE = 128
C = 256
DC = 512
FFN = 2048
S_DEV = 8
E_DEV = 1024
CC = 256
GROUPS = 16
HC = CC // GROUPS
ROWS = HC * 128
eps_norm = 1e-05
bf16 = jnp.bfloat16
f32 = jnp.float32
vm = pl.BlockSpec(memory_space=pltpu.VMEM)
hbm = pl.BlockSpec(memory_space=pltpu.HBM)


def dot(a, b):
    return jnp.dot(a, b, preferred_element_type=f32)


def gelu(x):
    scaled = (0.7978845608028654 * x).astype(bf16)
    short = x.astype(bf16)
    inner = scaled + scaled * (short * short * jnp.bfloat16(0.044715))
    half = short * jnp.bfloat16(0.5)
    return half + half * jnp.tanh(inner)


def pick_rows(ids_row, width=2 * TILE):
    across = jnp.broadcast_to(ids_row, (TILE, TILE)).astype(f32)
    down = across.T.astype(jnp.int32)
    lanes = lax.broadcasted_iota(jnp.int32, (TILE, TILE), 1)
    parts = [(down == lanes + TILE * i).astype(f32).astype(bf16) for i in range(width // TILE)]
    return jnp.concatenate(parts, axis=1)


def prepare_kernel(
    nbr_h, own_h, x_h, w1_h, w2_h, x, w1, w2, pick, hot, unpool, share, nbr, own, sems
):
    pairs = ((nbr_h, nbr), (own_h, own), (w1_h, w1), (w2_h, w2)) + tuple(
        (x_h.at[s], x.at[s]) for s in range(S_DEV)
    )
    copies = [pltpu.make_async_copy(src, dst, sems.at[i]) for i, (src, dst) in enumerate(pairs)]
    for copy in copies:
        copy.start()
    copies[0].wait()
    copies[1].wait()
    patch = lax.axis_index("patch")
    for j in range(8):
        for k in range(1, 5):
            ids = nbr[k : k + 1, j * TILE : (j + 1) * TILE] - (patch * E_DEV + j * TILE - HALO)
            pick[j, (k - 1) * TILE : k * TILE, :] = pick_rows(ids)
    slots = own[...] - patch * CC
    for j in range(8):
        unpool[j * TILE : (j + 1) * TILE, :] = pick_rows(slots[:, j * TILE : (j + 1) * TILE])
    rows = lax.broadcasted_iota(jnp.int32, (CC, E_DEV), 0)
    onehot = (rows == slots).astype(f32)
    hot[...] = onehot.astype(bf16)
    share[...] = jnp.broadcast_to(1.0 / jnp.sum(onehot, axis=1, keepdims=True), (CC, TILE))
    for copy in copies[2:]:
        copy.wait()


def prepare(nbr_t, own, x, w1, w2):
    return pl.pallas_call(
        prepare_kernel,
        in_specs=[hbm] * 5,
        out_specs=[vm] * 7,
        out_shape=[
            pltpu.VMEM((S_DEV, E_DEV, C), bf16),
            pltpu.VMEM((5 * C, C), bf16),
            pltpu.VMEM((C, C), bf16),
            pltpu.VMEM((8, 4 * TILE, 2 * TILE), bf16),
            pltpu.VMEM((CC, E_DEV), bf16),
            jax.ShapeDtypeStruct((E_DEV, CC), bf16),
            pltpu.VMEM((CC, TILE), f32),
        ],
        scratch_shapes=[
            pltpu.VMEM((5, E_DEV), jnp.int32),
            pltpu.VMEM((1, E_DEV), jnp.int32),
            pltpu.SemaphoreType.DMA((S_DEV + 4,)),
        ],
        compiler_params=pltpu.CompilerParams(vmem_limit_bytes=16 * 2**20),
        cost_estimate=pl.CostEstimate(flops=10**9, bytes_accessed=5 * 2**20, transcendentals=0),
        name="prepare",
    )(in_hbm(nbr_t), in_hbm(own), in_hbm(x), in_hbm(w1), in_hbm(w2))


def mix_kernel(x, w1, w2, pick, hot, share, before, after, mixed, send, gath, *sums):
    def gather(s, base):
        for j in range(8):
            if j == 0:
                window = jnp.concatenate([before[s], x[s, 0 : TILE + HALO]], axis=0)
            elif j == 7:
                window = jnp.concatenate([x[s, E_DEV - TILE - HALO :], after[s]], axis=0)
            else:
                window = x[s, j * TILE - HALO : j * TILE + TILE + HALO]
            got = dot(pick[j], window).astype(bf16)
            to = slice(base + j * TILE, base + (j + 1) * TILE)
            for k in range(4):
                gath[to, k * C : (k + 1) * C] = got[k * TILE : (k + 1) * TILE]

    def snapshots(b, _):
        for i in range(SB):
            gather(b * SB + i, i * E_DEV)
        centre = x[pl.ds(b * SB, SB)].reshape(SB * E_DEV, C)
        pre = dot(centre, w1[0:C, :]) + dot(gath[...], w1[C:, :])
        act = gelu(pre)
        both = (centre.astype(f32) + dot(act, w2[...])).astype(bf16)
        mixed[pl.ds(b * SB, SB)] = both.reshape(SB, E_DEV, C)
        for i in range(SB):
            total = dot(hot[...], both[i * E_DEV : (i + 1) * E_DEV])
            for h in range(2):
                mean = total[:, h * TILE : (h + 1) * TILE] * share[...]
                sums[h][pl.ds(b * SB + i, CC, stride=S_DEV), :] = mean
        return 0

    lax.fori_loop(0, S_DEV // SB, snapshots, 0)
    for g in range(GROUPS):
        for i in range(2):
            send[g, :, i * TILE : (i + 1) * TILE] = sums[i][
                g * HC * S_DEV : (g + 1) * HC * S_DEV, :
            ].astype(bf16)


SB = 2


def mix(x, w1, w2, pick, hot, share, before, after):
    return pl.pallas_call(
        mix_kernel,
        in_specs=[vm] * 8,
        out_specs=[vm] * 2,
        out_shape=[
            jax.ShapeDtypeStruct((S_DEV, E_DEV, C), bf16),
            jax.ShapeDtypeStruct((GROUPS, HC * S_DEV, C), bf16),
        ],
        scratch_shapes=[
            pltpu.VMEM((SB * E_DEV, 4 * C), bf16),
            pltpu.VMEM((CC * S_DEV, TILE), f32),
            pltpu.VMEM((CC * S_DEV, TILE), f32),
        ],
        compiler_params=pltpu.CompilerParams(vmem_limit_bytes=26 * 2**20),
        cost_estimate=pl.CostEstimate(flops=12 * 10**9, bytes_accessed=2**20, transcendentals=2**21),
        name="mix",
    )(x, w1, w2, pick, hot, share, before, after)


RB = 1024
FB = 256


def rms(rows, gain):
    mean_sq = jnp.mean(rows * rows, axis=-1, keepdims=True)
    return (rows * lax.rsqrt(mean_sq + eps_norm) * gain).astype(bf16)


def layer_kernel(
    x, ga, gf, lift, wqkv, wout, gate, up, down, dec, y,
    flat, qkv, lifted, att, normed, acc, hidden,
):
    for g in range(GROUPS):
        part = x[g].astype(f32)
        for c in range(HC):
            flat[c * 128 + g * S_DEV : c * 128 + (g + 1) * S_DEV, :] = part[c * S_DEV : (c + 1) * S_DEV]
    lane = lax.broadcasted_iota(jnp.int32, (128, 256), 1) // 64
    causal = lax.broadcasted_iota(jnp.int32, (512, 128), 1) <= (
        lax.broadcasted_iota(jnp.int32, (512, 128), 0) % 128
    )

    def block(b, _):
        r0 = b * RB
        if not isinstance(b, int):
            r0 = pl.multiple_of(r0, RB)

        rows = flat[pl.ds(r0, RB), :].astype(bf16)
        low = dot(rows, lift[...]).astype(bf16)
        lifted[...] = low
        normed[...] = rms(low.astype(f32), ga[...])
        qkv[...] = dot(normed[...], wqkv[...]).astype(bf16)
        for c in range(RB // 128):
            sl = slice(c * 128, (c + 1) * 128)
            for half in range(2):
                q = qkv[sl, half * 256 : half * 256 + 256].astype(f32) * 0.125
                k = qkv[sl, DC + half * 256 : DC + half * 256 + 256]
                v = qkv[sl, 2 * DC + half * 256 : 2 * DC + half * 256 + 256]
                stacked = jnp.concatenate(
                    [jnp.where(lane == h, q, 0.0).astype(bf16) for h in range(4)], axis=0
                )
                scores = lax.dot_general(
                    stacked, k, (((1,), (1,)), ((), ())), preferred_element_type=f32
                )
                scores = jnp.where(causal, scores, -jnp.inf)
                top = jnp.max(scores, axis=-1, keepdims=True)
                e = jnp.exp(scores - top)
                share = 1.0 / jnp.sum(e, axis=-1, keepdims=True)
                full = dot(e.astype(bf16), v) * share
                o = full[0:128]
                for h in range(1, 4):
                    o = jnp.where(lane == h, full[h * 128 : (h + 1) * 128], o)
                att[sl, half * 256 : half * 256 + 256] = o.astype(bf16)
        one = (lifted[...].astype(f32) + dot(att[...], wout[...])).astype(bf16).astype(f32)
        acc[...] = one
        normed[...] = rms(one, gf[...])
        for n in range(FFN // FB):
            cols = slice(n * FB, (n + 1) * FB)
            g = dot(normed[...], gate[:, cols])
            u = dot(normed[...], up[:, cols])
            hidden[:, cols] = (g * (1.0 / (1.0 + jnp.exp(-g))) * u).astype(bf16)
        two = (acc[...] + dot(hidden[...], down[...])).astype(bf16)
        flat[pl.ds(r0, RB), :] = dot(two, dec[...])
        return 0

    lax.fori_loop(0, ROWS // RB, block, 0, unroll=True)
    for g in range(GROUPS):
        y[g] = jnp.concatenate(
            [flat[c * 128 + g * S_DEV : c * 128 + (g + 1) * S_DEV, :] for c in range(HC)], axis=0
        ).astype(bf16)


def layer(x, ga, gf, weights):
    return pl.pallas_call(
        layer_kernel,
        in_specs=[vm] * 10,
        out_specs=vm,
        out_shape=jax.ShapeDtypeStruct((GROUPS, HC * S_DEV, C), bf16),
        scratch_shapes=[
            pltpu.VMEM((ROWS, C), f32),
            pltpu.VMEM((RB, 3 * DC), bf16),
            pltpu.VMEM((RB, DC), bf16),
            pltpu.VMEM((RB, DC), bf16),
            pltpu.VMEM((RB, DC), bf16),
            pltpu.VMEM((RB, DC), f32),
            pltpu.VMEM((RB, FFN), bf16),
        ],
        compiler_params=pltpu.CompilerParams(vmem_limit_bytes=32 * 2**20),
        cost_estimate=pl.CostEstimate(flops=24 * 10**9, bytes_accessed=2**20, transcendentals=2**22),
        name="layer",
    )(x, ga, gf, *weights)


def spread_kernel(mixed, hot, back, out_h, stage, out_sems, *flat):
    def save(s):
        return pltpu.make_async_copy(stage.at[s], out_h.at[s], out_sems.at[s])

    for h in range(2):
        flat[h][...] = back[:, h * TILE : (h + 1) * TILE].astype(f32)
    for s in range(S_DEV):
        coarse = jnp.concatenate(
            [flat[h][pl.ds(s, CC, stride=S_DEV), :].astype(bf16) for h in range(2)], axis=1
        )
        stage[s] = (mixed[s].astype(f32) + dot(hot[...], coarse)).astype(bf16)
        save(s).start()
    for s in range(S_DEV):
        save(s).wait()


def spread(mixed, hot, back):
    return pl.pallas_call(
        spread_kernel,
        in_specs=[vm, vm, vm],
        out_specs=hbm,
        out_shape=jax.ShapeDtypeStruct((S_DEV, E_DEV, C), bf16),
        scratch_shapes=[
            pltpu.VMEM((S_DEV, E_DEV, C), bf16),
            pltpu.SemaphoreType.DMA((S_DEV,)),
            pltpu.VMEM((ROWS, TILE), f32),
            pltpu.VMEM((ROWS, TILE), f32),
        ],
        compiler_params=pltpu.CompilerParams(vmem_limit_bytes=24 * 2**20),
        cost_estimate=pl.CostEstimate(flops=10**9, bytes_accessed=8 * 2**20, transcendentals=0),
        name="spread",
    )(mixed, hot, back)


def in_hbm(array):
    return pltpu.with_memory_space_constraint(array, pltpu.HBM)


def exchange(x):
    return lax.all_to_all(x, "tm", split_axis=0, concat_axis=0, tiled=True)


def per_device(
    snapshots, neighbours, owners, w_mix1, w_mix2, w_lift, gain_attn, w_qkv, w_out,
    gain_ffn, w_gate, w_up, w_down, w_dec,
):
    n_patch = lax.axis_size("patch")
    up = [(i, i + 1) for i in range(n_patch - 1)]
    down = [(j, i) for i, j in up]
    before = lax.ppermute(snapshots[:, E_DEV - HALO :], "patch", up)
    after = lax.ppermute(snapshots[:, :HALO], "patch", down)
    nbr_t = neighbours.T
    x, w1, w2, pick, hot, unpool, share = prepare(
        nbr_t, owners.reshape(1, E_DEV), snapshots, w_mix1, w_mix2
    )
    mixed, send = mix(x, w1, w2, pick, hot, share, before, after)
    weights = (w_lift, w_qkv, w_out, w_gate, w_up, w_down, w_dec)
    ga, gf = gain_attn.reshape(1, DC), gain_ffn.reshape(1, DC)
    back = exchange(layer(exchange(send), ga, gf, weights))
    return spread(mixed, unpool, back.reshape(ROWS, C))


def solution(mesh):
    in_specs = (P("tm", "patch", None), P("patch", None), P("patch")) + (P(),) * 11
    return jax.shard_map(
        per_device, mesh=mesh, in_specs=in_specs, out_specs=P("tm", "patch", None), check_vma=False
    )
```
